32 devices in a mesh: grp: 16 (over z, x, core), tp: 2 (over y).
Axes of the slice: x: 2, y: 2, z: 4, core: 2. Of those that a mesh axis runs over, the one named last changes fastest.
Arguments:
- activations: bfloat16 [4096, 5120], P('grp', 'tp'), may hold values from -6 to 6
- cotangent: bfloat16 [4096, 512], P('grp'), may hold values from -1.5 to 1.5
- advantage: int32 [16], replicated, may hold values from -512 to 512
- seq_len: int32 [16], replicated, may hold values from 64 to 256, as said below
- key_master: float32 [2, 2560, 512], P('tp', 'grp'), may hold values from -0.078125 to 0.078125
- moment_one: float32 [2, 2560, 512], P('tp', 'grp'), may hold values from -3 to 3
- moment_two: float32 [2, 2560, 512], P('tp', 'grp'), may hold values from 0.1 to 2
- decode_hidden: bfloat16 [16, 4, 5120], P('grp'), may hold values from -6 to 6
- queries: bfloat16 [16, 4, 2560], P('grp', None, 'tp'), may hold values from -34 to 34
- cache_keys: bfloat16 [16, 2048, 512], P('grp', None, 'tp'), may hold values from -6 to 6
- cache_values: bfloat16 [16, 2048, 512], P('grp', None, 'tp'), may hold values from -6 to 6
- cache_len: int32 [16], P('grp'), may hold values from 2 to 2048, as said below
- value_weight: bfloat16 [5120, 512], P(None, 'tp'), may hold values from -0.078125 to 0.078125
Outputs:
- master_new: float32 [2, 2560, 512], P('tp', 'grp')
- moment_one_new: float32 [2, 2560, 512], P('tp', 'grp')
- moment_two_new: float32 [2, 2560, 512], P('tp', 'grp')
- new_keys: bfloat16 [16, 4, 512], P('grp', None, 'tp')
- new_values: bfloat16 [16, 4, 512], P('grp', None, 'tp')
- attention: bfloat16 [16, 4, 2560], P('grp', None, 'tp')
The draws below stay inside these ranges and needn't reach their ends.
Inputs may be any that keep to these rules, and one draw needn't show every extreme that they name: `seq_len`: the first sequence is full. `cache_len`: row 0 has a full cache.
All inputs are finite; a program needn't handle non-finite values.
Results may differ from the reference program's by a relative error of at most 0.0044.
The reference program's roundings to bfloat16 on the way count: a program that leaves them out, or rounds other values in their place, can miss the bound.
Values may be sent and summed in bfloat16 or wider, within the bound.
A program may use at most 64 MiB of HBM per device.

```python
import math
import jax
import jax.numpy as jnp
from jax import lax

D = 5120
HD = 128
KVH = 4
GQA = 5
STEPS = 4
CACHE = 2048
SEQ = 256
QH = 20
KW = 512
DQ = 2560
DQPAD = 2560
TOKENS = 4096
NSEQ = 16
ROWS = 16
N_TP = 2


def shared_cache(key):
    base = jax.random.fold_in(key, 11)
    keys = jnp.clip(jax.random.normal(base, (ROWS, CACHE, KW), jnp.float32), -6.0, 6.0)
    return keys


def draw_cache_keys(key, part):
    return shared_cache(key).astype(jnp.bfloat16)


def draw_queries(key, part):
    own = jax.random.fold_in(key, 23)
    values = jnp.clip(jax.random.normal(own, (ROWS, STEPS, QH * HD), jnp.float32), -6.0, 6.0)
    return values.astype(jnp.bfloat16)


def draw_seq_len(key, part):
    lengths = jax.random.randint(jax.random.fold_in(key, 31), (NSEQ,), SEQ // 4, SEQ + 1)
    return lengths.at[0].set(SEQ).astype(jnp.int32)


def draw_cache_len(key, part):
    lengths = jax.random.randint(jax.random.fold_in(key, 37), (ROWS,), 2, CACHE + 1)
    return lengths.at[0].set(CACHE).astype(jnp.int32)


def place_ends(values, own_key, least, largest):
    place = [jax.random.randint(jax.random.fold_in(own_key, axis), (), 0, length) for axis, length in enumerate(values.shape)]
    widest = values.shape.index(max(values.shape))
    neighbour = place[:widest] + [(place[widest] + 1) % values.shape[widest]] + place[widest + 1:]
    return values.at[tuple(place)].set(least).at[tuple(neighbour)].set(largest)


def strengthened(drawn, own_key, source, target, blocks, factor):
    def block_of(axis_at):
        return (jnp.arange(drawn.shape[axis_at]) // (drawn.shape[axis_at] // blocks)).reshape((-1,) + (1,) * (drawn.ndim - 1 - axis_at))

    first = jax.random.permutation(own_key, blocks)[block_of(target)]
    far = (block_of(target) + blocks // 2) % blocks
    return jnp.where((block_of(source) == first) | (block_of(source) == far), factor * drawn, drawn)


def block_scale(stream_key, shape, split, least, largest):
    def one(dim, shards_of):
        steps = jax.random.uniform(jax.random.fold_in(jax.random.fold_in(stream_key, 6), dim), (shards_of,), jnp.float32, least / len(split), largest / len(split))
        return jnp.repeat(jnp.exp(steps), shape[dim] // shards_of).reshape((-1,) + (1,) * (len(shape) - dim - 1))

    loudness = one(*split[0])
    for cut in split[1:]:
        loudness = loudness * one(*cut)
    return loudness


def noise(rng, extent, width, bound, split=(), held_as=jnp.bfloat16):
    result = width * jax.random.normal(rng, extent, jnp.float32)
    if split:
        result = result * block_scale(rng, extent, split, -0.22, 0.18)
    return jnp.clip(result, -bound, bound).astype(held_as)


def gaussian_with(key, dims, spread, bound, pieces, heavy, held_as=jnp.bfloat16):
    result = spread * jax.random.normal(key, dims, jnp.float32)
    if pieces:
        result = result * block_scale(key, dims, pieces, -0.22, 0.18)
    return jnp.clip(strengthened(result, jax.random.fold_in(key, 3), *heavy), -bound, bound).astype(held_as)


def setup_inputs(seed: int = 0) -> dict:
    arg_keys = jax.random.split(jax.random.key(seed), 14)
    return {
        "activations": gaussian_with(arg_keys[0], (TOKENS, D), 1.0, 6.0, ((0, 16), (1, 2)), (0, 1, 16, 2.0)),
        "cotangent": noise(arg_keys[1], (TOKENS, KW), 0.25, 1.5, ((0, 16),)),
        "advantage": place_ends(jax.random.randint(arg_keys[2], (NSEQ,), -512, 513), jax.random.fold_in(arg_keys[2], 1), -512, 512).astype(jnp.int32),
        "seq_len": draw_seq_len(jax.random.fold_in(arg_keys[13], 71), 0),
        "key_master": noise(arg_keys[4], (N_TP, DQPAD, KW), D ** -0.5, 0.078125, ((0, 2), (1, 16)), jnp.float32),
        "moment_one": noise(arg_keys[5], (N_TP, DQPAD, KW), 0.5, 3.0, ((0, 2), (1, 16)), jnp.float32),
        "moment_two": jnp.clip(jnp.exp(math.log(2.0) - 2.9957323 * jax.random.uniform(arg_keys[6], (N_TP, DQPAD, KW), jnp.float32) ** block_scale(arg_keys[6], (N_TP, DQPAD, KW), ((0, 2), (1, 16)), -0.2, 0.2)), 0.1, 2.0),
        "decode_hidden": noise(arg_keys[7], (ROWS, STEPS, D), 1.0, 6.0, ((0, 16),)),
        "queries": draw_queries(jax.random.fold_in(arg_keys[13], 71), 0),
        "cache_keys": draw_cache_keys(jax.random.fold_in(arg_keys[13], 71), 0),
        "cache_values": noise(arg_keys[10], (ROWS, CACHE, KW), 1.0, 6.0, ((0, 16), (2, 2))),
        "cache_len": draw_cache_len(jax.random.fold_in(arg_keys[13], 71), 0),
        "value_weight": noise(arg_keys[12], (D, KW), D ** -0.5, 0.078125, ((1, 2),)),
    }


def reference(activations, cotangent, advantage, seq_len, key_master, moment_one, moment_two, decode_hidden, queries, cache_keys, cache_values, cache_len, value_weight):
    position = jnp.arange(TOKENS, dtype=jnp.int32)
    seq_index = position // SEQ
    within = position % SEQ
    length_tok = seq_len[seq_index]
    adv_tok = advantage[seq_index].astype(jnp.float32) / 256.0
    scale = jnp.where(within < length_tok, adv_tok, jnp.float32(0.0)) / NSEQ
    weighted = (cotangent.astype(jnp.float32) * scale[:, None]).astype(jnp.bfloat16)
    gradient = jnp.dot(activations.T, weighted, preferred_element_type=jnp.float32)
    grad_blocks = gradient.reshape(N_TP, DQ, KW)
    grad_blocks = jnp.concatenate([grad_blocks, jnp.zeros((N_TP, DQPAD - DQ, KW), jnp.float32)], axis=1)
    corr_one = 1.0 - 0.9 ** 10
    corr_two = 1.0 - 0.95 ** 10
    moment_one_new = 0.9 * moment_one + 0.1 * grad_blocks
    moment_two_new = 0.95 * moment_two + 0.05 * grad_blocks * grad_blocks
    master_new = key_master - 0.005 * (moment_one_new / corr_one) / (jnp.sqrt(moment_two_new / corr_two) + 1e-08)
    relayed = master_new.astype(jnp.bfloat16)[:, :DQ, :].reshape(D, KW)
    flat_hidden = decode_hidden.reshape(ROWS * STEPS, D)
    new_keys = jnp.dot(flat_hidden, relayed, preferred_element_type=jnp.float32).astype(jnp.bfloat16).reshape(ROWS, STEPS, KW)
    new_values = jnp.dot(flat_hidden, value_weight, preferred_element_type=jnp.float32).astype(jnp.bfloat16).reshape(ROWS, STEPS, KW)
    inverse = 1.0 / math.sqrt(HD)
    shaped_q = queries.astype(jnp.float32).reshape(ROWS, STEPS, KVH, GQA, HD)
    keys_c = cache_keys.astype(jnp.float32).reshape(ROWS, CACHE, KVH, HD)
    vals_c = cache_values.astype(jnp.float32).reshape(ROWS, CACHE, KVH, HD)
    keys_n = new_keys.astype(jnp.float32).reshape(ROWS, STEPS, KVH, HD)
    vals_n = new_values.astype(jnp.float32).reshape(ROWS, STEPS, KVH, HD)
    score_c = jnp.einsum('rsgqd,rcgd->rgsqc', shaped_q, keys_c) * inverse
    score_n = jnp.einsum('rsgqd,rtgd->rgsqt', shaped_q, keys_n) * inverse
    valid = jnp.arange(CACHE, dtype=jnp.int32)[None, :] < cache_len[:, None]
    score_c = jnp.where(valid[:, None, None, None, :], score_c, -jnp.inf)
    causal = jnp.arange(STEPS, dtype=jnp.int32)[None, :] <= jnp.arange(STEPS, dtype=jnp.int32)[:, None]
    score_n = jnp.where(causal[None, None, :, None, :], score_n, -jnp.inf)
    top = jnp.maximum(lax.optimization_barrier(jnp.max(score_c, axis=-1)), lax.optimization_barrier(jnp.max(score_n, axis=-1)))
    exp_c = jnp.exp(score_c - top[..., None])
    exp_n = jnp.exp(score_n - top[..., None])
    total = lax.optimization_barrier(jnp.sum(exp_c, axis=-1)) + lax.optimization_barrier(jnp.sum(exp_n, axis=-1))
    probs_c = (exp_c / total[..., None]).astype(jnp.bfloat16).astype(jnp.float32)
    probs_n = (exp_n / total[..., None]).astype(jnp.bfloat16).astype(jnp.float32)
    mixed = jnp.einsum('rgsqc,rcgd->rsgqd', probs_c, vals_c) + jnp.einsum('rgsqt,rtgd->rsgqd', probs_n, vals_n)
    attention = mixed.astype(jnp.bfloat16).reshape(ROWS, STEPS, QH * HD)
    return (master_new, moment_one_new, moment_two_new, new_keys, new_values, attention)
```

```python
import functools
import math

import jax
import jax.numpy as jnp
from jax import lax
from jax.experimental import pallas as pl
from jax.experimental.pallas import tpu as pltpu
from jax.sharding import PartitionSpec as P

HD = 128
GQA = 5
SEQ = 256


def attend(queries, cache_keys, cache_values, cache_len, new_keys, new_values):
    rows, steps, width = queries.shape
    length = cache_keys.shape[1]
    heads_kv = cache_keys.shape[2] // HD
    inverse = 1.0 / math.sqrt(HD)
    shaped_q = queries.reshape(rows, steps, heads_kv, GQA, HD)
    keys_c = cache_keys.reshape(rows, length, heads_kv, HD)
    vals_c = cache_values.reshape(rows, length, heads_kv, HD)
    keys_n = new_keys.reshape(rows, steps, heads_kv, HD)
    vals_n = new_values.reshape(rows, steps, heads_kv, HD)
    score_c = (
        jnp.einsum("rsgqd,rcgd->rgsqc", shaped_q, keys_c, preferred_element_type=jnp.float32)
        * inverse
    )
    score_n = (
        jnp.einsum("rsgqd,rtgd->rgsqt", shaped_q, keys_n, preferred_element_type=jnp.float32)
        * inverse
    )
    valid = jnp.arange(length, dtype=jnp.int32)[None, :] < cache_len[:, None]
    score_c = jnp.where(valid[:, None, None, None, :], score_c, -jnp.inf)
    causal = (
        jnp.arange(steps, dtype=jnp.int32)[None, :] <= jnp.arange(steps, dtype=jnp.int32)[:, None]
    )
    score_n = jnp.where(causal[None, None, :, None, :], score_n, -jnp.inf)
    top = jnp.maximum(jnp.max(score_c, axis=-1), jnp.max(score_n, axis=-1))
    exp_c = jnp.exp(score_c - top[..., None])
    exp_n = jnp.exp(score_n - top[..., None])
    total = jnp.sum(exp_c, axis=-1) + jnp.sum(exp_n, axis=-1)
    probs_c = (exp_c / total[..., None]).astype(jnp.bfloat16)
    probs_n = (exp_n / total[..., None]).astype(jnp.bfloat16)
    mixed = jnp.einsum("rgsqc,rcgd->rsgqd", probs_c, vals_c, preferred_element_type=jnp.float32)
    mixed = mixed + jnp.einsum(
        "rgsqt,rtgd->rsgqd", probs_n, vals_n, preferred_element_type=jnp.float32
    )
    return mixed.astype(jnp.bfloat16).reshape(rows, steps, width)


def plain_shards(
    activations,
    cotangent,
    advantage,
    seq_len,
    key_master,
    moment_one,
    moment_two,
    decode_hidden,
    queries,
    cache_keys,
    cache_values,
    cache_len,
    value_weight,
):
    tok_rows = activations.shape[0]
    quarter_rows = activations.shape[1]
    groups = lax.axis_size("grp")
    sequences = seq_len.shape[0]
    position = lax.axis_index("grp") * tok_rows + jnp.arange(tok_rows, dtype=jnp.int32)
    seq_index = position // SEQ
    within = position % SEQ
    onehot = seq_index[:, None] == jnp.arange(sequences, dtype=jnp.int32)[None, :]
    length_tok = jnp.sum(jnp.where(onehot, seq_len[None, :], 0), axis=1)
    adv_tok = jnp.sum(jnp.where(onehot, advantage[None, :], 0), axis=1).astype(jnp.float32) / 256.0
    scale = jnp.where(within < length_tok, adv_tok, jnp.float32(0.0)) / sequences
    weighted = (cotangent.astype(jnp.float32) * scale[:, None]).astype(jnp.bfloat16)
    own_rows = key_master.shape[1]
    padded = jnp.pad(activations, ((0, 0), (0, own_rows * groups - quarter_rows)))
    gradient = lax.psum_scatter(
        lax.dot_general(
            padded, weighted, (((0,), (0,)), ((), ())), preferred_element_type=jnp.float32
        ),
        "grp",
        scatter_dimension=0,
        tiled=True,
    )
    gradient = gradient.reshape(key_master.shape)
    corr_one = 1.0 - 0.9**10
    corr_two = 1.0 - 0.95**10
    moment_one_new = 0.9 * moment_one + 0.1 * gradient
    moment_two_new = 0.95 * moment_two + 0.05 * gradient * gradient
    master_new = key_master - 0.005 * (moment_one_new / corr_one) / (
        jnp.sqrt(moment_two_new / corr_two) + 1e-08
    )
    relay = master_new.astype(jnp.bfloat16)
    pieces = lax.all_to_all(relay, "tp", split_axis=2, concat_axis=0, tiled=True)
    columns = lax.all_gather(pieces, "grp", axis=1, tiled=True)
    weight_cols = columns[:, :quarter_rows].reshape(-1, columns.shape[2])
    rows, steps, width = decode_hidden.shape
    flat_hidden = decode_hidden.reshape(rows * steps, width)
    new_keys = (
        jnp.dot(flat_hidden, weight_cols, preferred_element_type=jnp.float32)
        .astype(jnp.bfloat16)
        .reshape(rows, steps, -1)
    )
    new_values = (
        jnp.dot(flat_hidden, value_weight, preferred_element_type=jnp.float32)
        .astype(jnp.bfloat16)
        .reshape(rows, steps, -1)
    )
    attention = attend(queries, cache_keys, cache_values, cache_len, new_keys, new_values)
    return (master_new, moment_one_new, moment_two_new, new_keys, new_values, attention)


MESH = pl.DeviceIdType.MESH
F32 = jnp.float32
BF16 = jnp.bfloat16


def fused(
    dims,
    act_ref, cot_ref, adv_ref, len_ref, master_ref, one_ref, two_ref, hid_ref, hid_own_ref,
    dec_ref, query_ref, ck_ref, cv_ref, clen_ref, vw_ref,
    master_out, one_out, two_out, keys_out, values_out, att_out,
    part, core_in, acc, x_out, x_in, z_out, z_in,
    hid, hid_rows, spread, y_part, y_core, y_x, y_xin, y_z, y_zin, y_t, y_tin,
    ck, cv, vw, q_rows, scores, new_k, new_v, rows16, att,
    local_sem, core_sem, x_sem, z_sem, hz_sem, hx_sem, yc_sem, yz_sem, yt_sem,
):
    groups, tps, steps = dims
    depth = groups // 4
    me = lax.axis_index("grp")
    t = lax.axis_index("tp")
    core = lax.rem(me, 2)
    x = lax.rem(lax.div(me, 2), 2)
    z = lax.div(me, 4)
    other_core, other_x = 1 - core, 1 - x
    core_dev = (z * 4 + x * 2 + other_core, t)
    x_dev = (z * 4 + other_x * 2 + core, t)

    def z_dev(j):
        return (lax.rem(z + j, depth) * 4 + x * 2 + core, t)

    def t_dev(i):
        return (me, lax.rem(t + i, tps))

    partners = [core_dev, x_dev]
    partners += [z_dev(j) for j in range(1, depth)] + [t_dev(i) for i in range(1, tps)]
    sent = []

    def remote(src, dst, sems, slot, device):
        return pltpu.make_async_remote_copy(
            src_ref=src, dst_ref=dst, send_sem=sems.at[0, slot], recv_sem=sems.at[1, slot],
            device_id=device, device_id_type=MESH,
        )

    def send(copy):
        copy.start()
        sent.append(copy)
        return copy

    load_k = pltpu.make_async_copy(ck_ref, ck, local_sem.at[0])
    load_v = pltpu.make_async_copy(cv_ref, cv, local_sem.at[1])
    load_w = pltpu.make_async_copy(vw_ref, vw, local_sem.at[2])
    load_k.start()
    load_v.start()
    load_w.start()

    barrier = pltpu.get_barrier_semaphore()
    for device in partners:
        pl.semaphore_signal(barrier, inc=1, device_id=device, device_id_type=MESH)

    tokens, width = act_ref.shape
    sequences = len_ref.shape[1]
    position = me * tokens + lax.broadcasted_iota(jnp.int32, (tokens, sequences), 0)
    which = lax.broadcasted_iota(jnp.int32, (tokens, sequences), 1)
    mine = lax.div(position, SEQ) == which
    length = jnp.sum(jnp.where(mine, len_ref[...].astype(F32), 0.0), axis=1, keepdims=True)
    advantage = jnp.sum(jnp.where(mine, adv_ref[...].astype(F32), 0.0), axis=1, keepdims=True)
    within = lax.rem(
        me * tokens + lax.broadcasted_iota(jnp.int32, (tokens, 1), 0), SEQ
    ).astype(F32)
    scale = jnp.where(within < length, advantage / 256.0, 0.0) / sequences
    weighted = (cot_ref[...].astype(F32) * scale).astype(BF16)

    chunk = width // depth
    own = chunk // 4
    kw = cot_ref.shape[1]
    order = list(range(1, depth)) + [0]

    core_copies = {}
    waited = False
    for j in order:
        at = pl.multiple_of(lax.rem(z + j, depth) * chunk, 128)
        product = lax.dot_general(
            act_ref[:, pl.ds(at, chunk)], weighted, (((0,), (0,)), ((), ())),
            preferred_element_type=F32,
        )
        part[j] = product.reshape(2, 2, own, kw)
        if not waited:
            pl.semaphore_wait(barrier, len(partners))
            waited = True
        core_copies[j] = send(
            remote(part.at[j, :, other_core], core_in.at[j], core_sem, j, core_dev)
        )

    hid[0, 0, 0] = hid_own_ref[...]
    hid_z = [
        send(remote(hid_ref.at[lax.rem(z + j, depth)], hid.at[0, 0, j], hz_sem, j, z_dev(j)))
        for j in range(1, depth)
    ]

    x_copies = {}
    for j in order:
        core_copies[j].wait_recv()
        x_out[j] = (part[j, other_x, core] + core_in[j, other_x]).astype(BF16)
        x_copies[j] = send(remote(x_out.at[j], x_in.at[j], x_sem, j, x_dev))
        acc[j] = part[j, x, core] + core_in[j, x]

    heads = ck.shape[1] // HD
    gqa = GQA
    for copy in hid_z:
        copy.wait_recv()
    hid_x = send(remote(hid.at[0, 0], hid.at[0, 1], hx_sem, 0, x_dev))

    inverse = 1.0 / math.sqrt(HD)
    cached = ck.shape[0]
    q_rows[...] = jnp.zeros_like(q_rows)
    query = query_ref[...].astype(F32)
    for h in range(heads * gqa):
        q_rows[h // gqa, pl.ds((h % gqa) * steps, steps)] = query[:, h * HD : (h + 1) * HD]

    def cache_scores(g):
        scores[g, :, pl.ds(0, cached)] = lax.dot_general(
            q_rows[g].astype(BF16), ck[:, g * HD : (g + 1) * HD], (((1,), (1,)), ((), ())),
            preferred_element_type=F32,
        )


    def project_values():
        load_w.wait()
        rows16[...] = jnp.zeros_like(rows16)
        rows16[pl.ds(0, steps)] = jnp.dot(dec_ref[...], vw[...], preferred_element_type=F32)
        new_v[...] = jnp.zeros_like(new_v)
        new_v[pl.ds(0, 16)] = rows16[...].astype(BF16)
        values_out[...] = rows16[pl.ds(0, steps)].astype(BF16)

    load_k.wait()
    z_copies = []
    for turn, j in enumerate(order):
        if turn < heads:
            cache_scores(turn)
        if turn == len(order) - 1:
            for g in range(len(order), heads):
                cache_scores(g)
            project_values()
        x_copies[j].wait_recv()
        total = acc[j] + x_in[j].astype(F32)
        if j == 0:
            acc[0] = total
        else:
            z_out[j - 1] = total.astype(BF16)
            z_copies.append(
                send(remote(z_out.at[j - 1], z_in.at[j - 1], z_sem, j - 1, z_dev(j)))
            )
    hid_x.wait_recv()
    hid_core = send(remote(hid.at[0], hid.at[1], hx_sem, 1, core_dev))
    hid_core.wait_recv()
    for c in range(2):
        for b in range(2):
            for j in range(depth):
                at = ((c * 2 + b) * depth + j) * steps
                hid_rows[pl.ds(at, steps)] = hid[c, b, j]
    spread[...] = jnp.zeros_like(spread)
    new_k[...] = jnp.zeros_like(new_k)

    for copy in z_copies:
        copy.wait_recv()
    gradient = acc[0]
    for j in range(1, depth):
        gradient = gradient + z_in[j - 1].astype(F32)

    corr_one = 1.0 - 0.9**10
    corr_two = 1.0 - 0.95**10
    one_new = 0.9 * one_ref[...] + 0.1 * gradient
    two_new = 0.95 * two_ref[...] + 0.05 * gradient * gradient
    master_new = master_ref[...] - 0.005 * (one_new / corr_one) / (
        jnp.sqrt(two_new / corr_two) + 1e-08
    )
    one_out[...] = one_new
    two_out[...] = two_new
    master_out[...] = master_new

    spread[pl.ds(pl.multiple_of((x * 2 + core) * own, 16), own)] = master_new.astype(BF16)
    product = jnp.dot(hid_rows[...].astype(BF16), spread[...], preferred_element_type=F32)
    half = product.shape[0] // 2
    y_part[...] = product[half:]
    copy = send(remote(y_part, y_core, yc_sem, 0, core_dev))
    copy.wait_recv()
    product = product[:half] + y_core[...]
    half = half // 2
    y_x[...] = product[half:]
    copy = send(remote(y_x, y_xin, yc_sem, 1, x_dev))
    copy.wait_recv()
    product = product[:half] + y_xin[...]
    copies = []
    for j in range(1, depth):
        y_z[j - 1] = product[j * steps : (j + 1) * steps]
        copies.append(
            send(remote(y_z.at[j - 1], y_zin.at[j - 1], yz_sem, j - 1, z_dev(depth - j)))
        )
    for copy in copies:
        copy.wait_recv()
    product = product[:steps]
    for j in range(1, depth):
        product = product + y_zin[j - 1]
    columns = kw // tps
    for i in range(tps):
        y_t[i] = product[:, i * columns : (i + 1) * columns]
    copies = [
        send(remote(y_t.at[lax.rem(t + i, tps)], y_tin.at[i - 1], yt_sem, i - 1, t_dev(i)))
        for i in range(1, tps)
    ]
    for copy in copies:
        copy.wait_recv()
    keys = y_t[t]
    for i in range(1, tps):
        keys = keys + y_tin[i - 1]
    rows16[...] = jnp.zeros_like(rows16)
    rows16[pl.ds(0, steps)] = keys
    keys_out[...] = keys.astype(BF16)
    new_k[pl.ds(0, 16)] = rows16[...].astype(BF16)

    load_v.wait()
    rows = q_rows.shape[1]
    column = lax.broadcasted_iota(jnp.int32, (rows, cached), 1)
    valid = column < clen_ref[0]
    step = lax.rem(lax.broadcasted_iota(jnp.int32, (rows, HD), 0), steps)
    causal = lax.broadcasted_iota(jnp.int32, (rows, HD), 1) <= step
    for g in range(heads):
        lanes = slice(g * HD, (g + 1) * HD)
        score_n = lax.dot_general(
            q_rows[g].astype(BF16), new_k[:, lanes], (((1,), (1,)), ((), ())),
            preferred_element_type=F32,
        )
        score_c = jnp.where(valid, scores[g] * inverse, -jnp.inf)
        score_n = jnp.where(causal, score_n * inverse, -jnp.inf)
        top = jnp.maximum(
            jnp.max(score_c, axis=1, keepdims=True), jnp.max(score_n, axis=1, keepdims=True)
        )
        exp_c = jnp.exp(score_c - top)
        exp_n = jnp.exp(score_n - top)
        total = jnp.sum(exp_c, axis=1, keepdims=True) + jnp.sum(exp_n, axis=1, keepdims=True)
        mixed = jnp.dot(
            (exp_c / total).astype(BF16), cv[:, lanes], preferred_element_type=F32
        ) + jnp.dot((exp_n / total).astype(BF16), new_v[:, lanes], preferred_element_type=F32)
        for i in range(gqa):
            at = (g * gqa + i) * HD
            att[:, at : at + HD] = mixed[i * steps : (i + 1) * steps]
    att_out[...] = att[...].astype(BF16)

    for copy in sent:
        copy.wait_send()


def fast_shards(
    activations,
    cotangent,
    advantage,
    seq_len,
    key_master,
    moment_one,
    moment_two,
    decode_hidden,
    queries,
    cache_keys,
    cache_values,
    cache_len,
    value_weight,
):
    groups, tps = lax.axis_size("grp"), lax.axis_size("tp")
    depth = groups // 4
    tokens, width = activations.shape
    own, kw = key_master.shape[1:]
    chunk = width // depth
    steps = decode_hidden.shape[1]
    cached, kv_cols = cache_keys.shape[1:]
    heads = kv_cols // HD
    hidden = decode_hidden.reshape(steps, -1)
    mine = lax.dynamic_slice_in_dim(hidden, lax.axis_index("tp") * width, width, 1)
    mine = mine.reshape(steps, depth, chunk).transpose(1, 0, 2).astype(F32)
    own_hidden = lax.dynamic_index_in_dim(mine, lax.axis_index("grp") // 4, 0, keepdims=False)
    q_pad = -(-GQA * steps // 16) * 16
    vmem = pl.BlockSpec(memory_space=pltpu.VMEM)
    anywhere = pl.BlockSpec(memory_space=pl.ANY)
    smem = pl.BlockSpec(memory_space=pltpu.SMEM)
    dma = pltpu.SemaphoreType.DMA
    rows = groups * steps
    outs = pl.pallas_call(
        functools.partial(fused, (groups, tps, steps)),
        out_shape=(
            jax.ShapeDtypeStruct((own, kw), F32),
            jax.ShapeDtypeStruct((own, kw), F32),
            jax.ShapeDtypeStruct((own, kw), F32),
            jax.ShapeDtypeStruct((steps, kv_cols), BF16),
            jax.ShapeDtypeStruct((steps, kv_cols), BF16),
            jax.ShapeDtypeStruct((steps, queries.shape[2]), BF16),
        ),
        in_specs=[vmem] * 11 + [anywhere, anywhere, smem, anywhere],
        out_specs=(vmem,) * 6,
        scratch_shapes=[
            pltpu.VMEM((depth, 2, 2, own, kw), F32),
            pltpu.VMEM((depth, 2, own, kw), F32),
            pltpu.VMEM((depth, own, kw), F32),
            pltpu.VMEM((depth, own, kw), BF16),
            pltpu.VMEM((depth, own, kw), BF16),
            pltpu.VMEM((depth - 1, own, kw), BF16),
            pltpu.VMEM((depth - 1, own, kw), BF16),
            pltpu.VMEM((2, 2, depth, steps, chunk), F32),
            pltpu.VMEM((rows, chunk), F32),
            pltpu.VMEM((chunk, kw), BF16),
            pltpu.VMEM((rows // 2, kw), F32),
            pltpu.VMEM((rows // 2, kw), F32),
            pltpu.VMEM((rows // 4, kw), F32),
            pltpu.VMEM((rows // 4, kw), F32),
            pltpu.VMEM((depth - 1, steps, kw), F32),
            pltpu.VMEM((depth - 1, steps, kw), F32),
            pltpu.VMEM((tps, steps, kw // tps), F32),
            pltpu.VMEM((tps - 1, steps, kw // tps), F32),
            pltpu.VMEM((cached, kv_cols), BF16),
            pltpu.VMEM((cached, kv_cols), BF16),
            pltpu.VMEM(value_weight.shape, BF16),
            pltpu.VMEM((heads, q_pad, HD), F32),
            pltpu.VMEM((heads, q_pad, cached), F32),
            pltpu.VMEM((HD, kv_cols), BF16),
            pltpu.VMEM((HD, kv_cols), BF16),
            pltpu.VMEM((16, kv_cols), F32),
            pltpu.VMEM((steps, queries.shape[2]), F32),
            dma((3,)),
            dma((2, depth)),
            dma((2, depth)),
            dma((2, depth)),
            dma((2, depth)),
            dma((2, 2)),
            dma((2, 2)),
            dma((2, depth)),
            dma((2, tps)),
        ],
        compiler_params=pltpu.CompilerParams(
            collective_id=0, has_side_effects=True, vmem_limit_bytes=56 * 1024 * 1024
        ),
        cost_estimate=pl.CostEstimate(
            flops=2 * tokens * width * kw, bytes_accessed=8 * width * kw, transcendentals=0
        ),
    )(
        activations,
        cotangent,
        advantage.reshape(1, -1),
        seq_len.reshape(1, -1),
        key_master[0],
        moment_one[0],
        moment_two[0],
        mine,
        own_hidden,
        hidden,
        queries[0],
        cache_keys[0],
        cache_values[0],
        cache_len,
        value_weight,
    )
    return tuple(out[None] for out in outs)


def fits(activations, key_master, decode_hidden, cache_keys, value_weight):
    groups, tps = lax.axis_size("grp"), lax.axis_size("tp")
    own = key_master.shape[1]
    return (
        groups % 4 == 0
        and groups >= 8
        and tps >= 2
        and own % 16 == 0
        and own * groups == activations.shape[1]
        and (4 * own) % 128 == 0
        and decode_hidden.shape[0] == 1
        and decode_hidden.shape[1] <= 16
        and cache_keys.shape[1] % 128 == 0
    )


def shards(*args):
    if fits(args[0], args[4], args[7], args[9], args[12]):
        return fast_shards(*args)
    return plain_shards(*args)


def solution(mesh):
    placed = (
        P("grp", "tp"),
        P("grp", None),
        P(),
        P(),
        P("tp", "grp", None),
        P("tp", "grp", None),
        P("tp", "grp", None),
        P("grp", None, None),
        P("grp", None, "tp"),
        P("grp", None, "tp"),
        P("grp", None, "tp"),
        P("grp"),
        P(None, "tp"),
    )
    return jax.shard_map(
        shards,
        mesh=mesh,
        in_specs=placed,
        out_specs=(
            P("tp", "grp", None),
            P("tp", "grp", None),
            P("tp", "grp", None),
            P("grp", None, "tp"),
            P("grp", None, "tp"),
            P("grp", None, "tp"),
        ),
        check_vma=False,
    )
```

```python
import functools
import math

import jax
import jax.numpy as jnp
from jax import lax
from jax.experimental import pallas as pl
from jax.experimental.pallas import tpu as pltpu
from jax.sharding import PartitionSpec as P

HD = 128
GQA = 5
SEQ = 256


def attend(queries, cache_keys, cache_values, cache_len, new_keys, new_values):
    rows, steps, width = queries.shape
    length = cache_keys.shape[1]
    heads_kv = cache_keys.shape[2] // HD
    inverse = 1.0 / math.sqrt(HD)
    shaped_q = queries.reshape(rows, steps, heads_kv, GQA, HD)
    keys_c = cache_keys.reshape(rows, length, heads_kv, HD)
    vals_c = cache_values.reshape(rows, length, heads_kv, HD)
    keys_n = new_keys.reshape(rows, steps, heads_kv, HD)
    vals_n = new_values.reshape(rows, steps, heads_kv, HD)
    score_c = (
        jnp.einsum("rsgqd,rcgd->rgsqc", shaped_q, keys_c, preferred_element_type=jnp.float32)
        * inverse
    )
    score_n = (
        jnp.einsum("rsgqd,rtgd->rgsqt", shaped_q, keys_n, preferred_element_type=jnp.float32)
        * inverse
    )
    valid = jnp.arange(length, dtype=jnp.int32)[None, :] < cache_len[:, None]
    score_c = jnp.where(valid[:, None, None, None, :], score_c, -jnp.inf)
    causal = (
        jnp.arange(steps, dtype=jnp.int32)[None, :] <= jnp.arange(steps, dtype=jnp.int32)[:, None]
    )
    score_n = jnp.where(causal[None, None, :, None, :], score_n, -jnp.inf)
    top = jnp.maximum(jnp.max(score_c, axis=-1), jnp.max(score_n, axis=-1))
    exp_c = jnp.exp(score_c - top[..., None])
    exp_n = jnp.exp(score_n - top[..., None])
    total = jnp.sum(exp_c, axis=-1) + jnp.sum(exp_n, axis=-1)
    probs_c = (exp_c / total[..., None]).astype(jnp.bfloat16)
    probs_n = (exp_n / total[..., None]).astype(jnp.bfloat16)
    mixed = jnp.einsum("rgsqc,rcgd->rsgqd", probs_c, vals_c, preferred_element_type=jnp.float32)
    mixed = mixed + jnp.einsum(
        "rgsqt,rtgd->rsgqd", probs_n, vals_n, preferred_element_type=jnp.float32
    )
    return mixed.astype(jnp.bfloat16).reshape(rows, steps, width)


def plain_shards(
    activations,
    cotangent,
    advantage,
    seq_len,
    key_master,
    moment_one,
    moment_two,
    decode_hidden,
    queries,
    cache_keys,
    cache_values,
    cache_len,
    value_weight,
):
    tok_rows = activations.shape[0]
    quarter_rows = activations.shape[1]
    groups = lax.axis_size("grp")
    sequences = seq_len.shape[0]
    position = lax.axis_index("grp") * tok_rows + jnp.arange(tok_rows, dtype=jnp.int32)
    seq_index = position // SEQ
    within = position % SEQ
    onehot = seq_index[:, None] == jnp.arange(sequences, dtype=jnp.int32)[None, :]
    length_tok = jnp.sum(jnp.where(onehot, seq_len[None, :], 0), axis=1)
    adv_tok = jnp.sum(jnp.where(onehot, advantage[None, :], 0), axis=1).astype(jnp.float32) / 256.0
    scale = jnp.where(within < length_tok, adv_tok, jnp.float32(0.0)) / sequences
    weighted = (cotangent.astype(jnp.float32) * scale[:, None]).astype(jnp.bfloat16)
    own_rows = key_master.shape[1]
    padded = jnp.pad(activations, ((0, 0), (0, own_rows * groups - quarter_rows)))
    gradient = lax.psum_scatter(
        lax.dot_general(
            padded, weighted, (((0,), (0,)), ((), ())), preferred_element_type=jnp.float32
        ),
        "grp",
        scatter_dimension=0,
        tiled=True,
    )
    gradient = gradient.reshape(key_master.shape)
    corr_one = 1.0 - 0.9**10
    corr_two = 1.0 - 0.95**10
    moment_one_new = 0.9 * moment_one + 0.1 * gradient
    moment_two_new = 0.95 * moment_two + 0.05 * gradient * gradient
    master_new = key_master - 0.005 * (moment_one_new / corr_one) / (
        jnp.sqrt(moment_two_new / corr_two) + 1e-08
    )
    relay = master_new.astype(jnp.bfloat16)
    pieces = lax.all_to_all(relay, "tp", split_axis=2, concat_axis=0, tiled=True)
    columns = lax.all_gather(pieces, "grp", axis=1, tiled=True)
    weight_cols = columns[:, :quarter_rows].reshape(-1, columns.shape[2])
    rows, steps, width = decode_hidden.shape
    flat_hidden = decode_hidden.reshape(rows * steps, width)
    new_keys = (
        jnp.dot(flat_hidden, weight_cols, preferred_element_type=jnp.float32)
        .astype(jnp.bfloat16)
        .reshape(rows, steps, -1)
    )
    new_values = (
        jnp.dot(flat_hidden, value_weight, preferred_element_type=jnp.float32)
        .astype(jnp.bfloat16)
        .reshape(rows, steps, -1)
    )
    attention = attend(queries, cache_keys, cache_values, cache_len, new_keys, new_values)
    return (master_new, moment_one_new, moment_two_new, new_keys, new_values, attention)


MESH = pl.DeviceIdType.MESH
F32 = jnp.float32
BF16 = jnp.bfloat16


def fused(
    dims,
    act_ref, cot_ref, adv_ref, len_ref, master_ref, one_ref, two_ref, hid_ref,
    dec_ref, query_ref, ck_ref, cv_ref, clen_ref, vw_ref,
    master_out, one_out, two_out, keys_out, values_out, att_out,
    part, core_in, acc, x_out, x_in, z_out, z_in,
    hid, hid_rows, spread, y_part, y_core, y_x, y_xin, y_z, y_zin, y_t, y_tin,
    ck, cv, vw, q_rows, scores, new_k, new_v, rows16, att,
    local_sem, core_sem, x_sem, z_sem, hz_sem, hx_sem, yc_sem, yz_sem, yt_sem,
):
    groups, tps, steps = dims
    depth = groups // 4
    me = lax.axis_index("grp")
    t = lax.axis_index("tp")
    core = lax.rem(me, 2)
    x = lax.rem(lax.div(me, 2), 2)
    z = lax.div(me, 4)
    other_core, other_x = 1 - core, 1 - x
    core_dev = (z * 4 + x * 2 + other_core, t)
    x_dev = (z * 4 + other_x * 2 + core, t)

    def z_dev(j):
        return (lax.rem(z + j, depth) * 4 + x * 2 + core, t)

    def t_dev(i):
        return (me, lax.rem(t + i, tps))

    partners = [core_dev, x_dev]
    partners += [z_dev(j) for j in range(1, depth)] + [t_dev(i) for i in range(1, tps)]
    sent = []

    def remote(src, dst, sems, slot, device):
        return pltpu.make_async_remote_copy(
            src_ref=src, dst_ref=dst, send_sem=sems.at[0, slot], recv_sem=sems.at[1, slot],
            device_id=device, device_id_type=MESH,
        )

    def send(copy):
        copy.start()
        sent.append(copy)
        return copy

    load_k = pltpu.make_async_copy(ck_ref, ck, local_sem.at[0])
    load_v = pltpu.make_async_copy(cv_ref, cv, local_sem.at[1])
    load_w = pltpu.make_async_copy(vw_ref, vw, local_sem.at[2])
    load_k.start()
    load_v.start()
    load_w.start()

    barrier = pltpu.get_barrier_semaphore()
    for device in partners:
        pl.semaphore_signal(barrier, inc=1, device_id=device, device_id_type=MESH)

    tokens, width = act_ref.shape
    sequences = len_ref.shape[1]
    position = me * tokens + lax.broadcasted_iota(jnp.int32, (tokens, sequences), 0)
    which = lax.broadcasted_iota(jnp.int32, (tokens, sequences), 1)
    mine = lax.div(position, SEQ) == which
    length = jnp.sum(jnp.where(mine, len_ref[...].astype(F32), 0.0), axis=1, keepdims=True)
    advantage = jnp.sum(jnp.where(mine, adv_ref[...].astype(F32), 0.0), axis=1, keepdims=True)
    within = lax.rem(
        me * tokens + lax.broadcasted_iota(jnp.int32, (tokens, 1), 0), SEQ
    ).astype(F32)
    scale = jnp.where(within < length, advantage / 256.0, 0.0) / sequences
    weighted = (cot_ref[...].astype(F32) * scale).astype(BF16)

    chunk = width // depth
    own = chunk // 4
    kw = cot_ref.shape[1]
    order = list(range(1, depth)) + [0]

    core_copies = {}
    waited = False
    for j in order:
        at = pl.multiple_of(lax.rem(z + j, depth) * chunk, 128)
        product = lax.dot_general(
            act_ref[:, pl.ds(at, chunk)], weighted, (((0,), (0,)), ((), ())),
            preferred_element_type=F32,
        )
        part[j] = product.reshape(2, 2, own, kw)
        if not waited:
            pl.semaphore_wait(barrier, len(partners))
            waited = True
        core_copies[j] = send(
            remote(part.at[j, :, other_core], core_in.at[j], core_sem, j, core_dev)
        )

    hid[0, 0, 0] = hid_ref[z]
    hid_z = [
        send(remote(hid_ref.at[lax.rem(z + j, depth)], hid.at[0, 0, j], hz_sem, j, z_dev(j)))
        for j in range(1, depth)
    ]

    x_copies = {}
    for j in order:
        core_copies[j].wait_recv()
        x_out[j] = (part[j, other_x, core] + core_in[j, other_x]).astype(BF16)
        x_copies[j] = send(remote(x_out.at[j], x_in.at[j], x_sem, j, x_dev))
        acc[j] = part[j, x, core] + core_in[j, x]

    heads = ck.shape[1] // HD
    gqa = GQA
    for copy in hid_z:
        copy.wait_recv()
    hid_x = send(remote(hid.at[0, 0], hid.at[0, 1], hx_sem, 0, x_dev))

    inverse = 1.0 / math.sqrt(HD)
    cached = ck.shape[0]
    q_rows[...] = jnp.zeros_like(q_rows)
    query = query_ref[...].astype(F32)
    for h in range(heads * gqa):
        q_rows[h // gqa, pl.ds((h % gqa) * steps, steps)] = query[:, h * HD : (h + 1) * HD]

    def cache_scores(g):
        scores[g, :, pl.ds(0, cached)] = lax.dot_general(
            q_rows[g].astype(BF16), ck[:, g * HD : (g + 1) * HD], (((1,), (1,)), ((), ())),
            preferred_element_type=F32,
        )


    def project_values():
        load_w.wait()
        rows16[...] = jnp.zeros_like(rows16)
        rows16[pl.ds(0, steps)] = jnp.dot(dec_ref[...], vw[...], preferred_element_type=F32)
        new_v[...] = jnp.zeros_like(new_v)
        new_v[pl.ds(0, 16)] = rows16[...].astype(BF16)
        values_out[...] = rows16[pl.ds(0, steps)].astype(BF16)

    load_k.wait()
    z_copies = []
    for turn, j in enumerate(order):
        if turn < heads:
            cache_scores(turn)
        if turn == len(order) - 1:
            for g in range(len(order), heads):
                cache_scores(g)
            project_values()
        x_copies[j].wait_recv()
        total = acc[j] + x_in[j].astype(F32)
        if j == 0:
            acc[0] = total
        else:
            z_out[j - 1] = total.astype(BF16)
            z_copies.append(
                send(remote(z_out.at[j - 1], z_in.at[j - 1], z_sem, j - 1, z_dev(j)))
            )
    hid_x.wait_recv()
    hid_core = send(remote(hid.at[0], hid.at[1], hx_sem, 1, core_dev))
    hid_core.wait_recv()
    for c in range(2):
        for b in range(2):
            for j in range(depth):
                at = ((c * 2 + b) * depth + j) * steps
                hid_rows[pl.ds(at, steps)] = hid[c, b, j]
    spread[...] = jnp.zeros_like(spread)
    new_k[...] = jnp.zeros_like(new_k)

    for copy in z_copies:
        copy.wait_recv()
    gradient = acc[0]
    for j in range(1, depth):
        gradient = gradient + z_in[j - 1].astype(F32)

    corr_one = 1.0 - 0.9**10
    corr_two = 1.0 - 0.95**10
    one_new = 0.9 * one_ref[...] + 0.1 * gradient
    two_new = 0.95 * two_ref[...] + 0.05 * gradient * gradient
    master_new = master_ref[...] - 0.005 * (one_new / corr_one) / (
        jnp.sqrt(two_new / corr_two) + 1e-08
    )
    one_out[...] = one_new
    two_out[...] = two_new
    master_out[...] = master_new

    spread[pl.ds(pl.multiple_of((x * 2 + core) * own, 16), own)] = master_new.astype(BF16)
    product = jnp.dot(hid_rows[...].astype(BF16), spread[...], preferred_element_type=F32)
    half = product.shape[0] // 2
    y_part[...] = product[half:]
    copy = send(remote(y_part, y_core, yc_sem, 0, core_dev))
    copy.wait_recv()
    product = product[:half] + y_core[...]
    half = half // 2
    y_x[...] = product[half:]
    copy = send(remote(y_x, y_xin, yc_sem, 1, x_dev))
    copy.wait_recv()
    product = product[:half] + y_xin[...]
    copies = []
    for j in range(1, depth):
        y_z[j - 1] = product[j * steps : (j + 1) * steps]
        copies.append(
            send(remote(y_z.at[j - 1], y_zin.at[j - 1], yz_sem, j - 1, z_dev(depth - j)))
        )
    for copy in copies:
        copy.wait_recv()
    product = product[:steps]
    for j in range(1, depth):
        product = product + y_zin[j - 1]
    columns = kw // tps
    for i in range(tps):
        y_t[i] = product[:, i * columns : (i + 1) * columns]
    copies = [
        send(remote(y_t.at[lax.rem(t + i, tps)], y_tin.at[i - 1], yt_sem, i - 1, t_dev(i)))
        for i in range(1, tps)
    ]
    for copy in copies:
        copy.wait_recv()
    keys = y_t[t]
    for i in range(1, tps):
        keys = keys + y_tin[i - 1]
    rows16[...] = jnp.zeros_like(rows16)
    rows16[pl.ds(0, steps)] = keys
    keys_out[...] = keys.astype(BF16)
    new_k[pl.ds(0, 16)] = rows16[...].astype(BF16)

    load_v.wait()
    rows = q_rows.shape[1]
    column = lax.broadcasted_iota(jnp.int32, (rows, cached), 1)
    valid = column < clen_ref[0]
    step = lax.rem(lax.broadcasted_iota(jnp.int32, (rows, HD), 0), steps)
    causal = lax.broadcasted_iota(jnp.int32, (rows, HD), 1) <= step
    for g in range(heads):
        lanes = slice(g * HD, (g + 1) * HD)
        score_n = lax.dot_general(
            q_rows[g].astype(BF16), new_k[:, lanes], (((1,), (1,)), ((), ())),
            preferred_element_type=F32,
        )
        score_c = jnp.where(valid, scores[g] * inverse, -jnp.inf)
        score_n = jnp.where(causal, score_n * inverse, -jnp.inf)
        top = jnp.maximum(
            jnp.max(score_c, axis=1, keepdims=True), jnp.max(score_n, axis=1, keepdims=True)
        )
        exp_c = jnp.exp(score_c - top)
        exp_n = jnp.exp(score_n - top)
        total = jnp.sum(exp_c, axis=1, keepdims=True) + jnp.sum(exp_n, axis=1, keepdims=True)
        mixed = jnp.dot(
            (exp_c / total).astype(BF16), cv[:, lanes], preferred_element_type=F32
        ) + jnp.dot((exp_n / total).astype(BF16), new_v[:, lanes], preferred_element_type=F32)
        for i in range(gqa):
            at = (g * gqa + i) * HD
            att[:, at : at + HD] = mixed[i * steps : (i + 1) * steps]
    att_out[...] = att[...].astype(BF16)

    for copy in sent:
        copy.wait_send()


def hand_over(*refs):
    half = len(refs) // 2
    for source, target in zip(refs[:half], refs[half:]):
        target[...] = source[...]


def fast_shards(
    activations,
    cotangent,
    advantage,
    seq_len,
    key_master,
    moment_one,
    moment_two,
    decode_hidden,
    queries,
    cache_keys,
    cache_values,
    cache_len,
    value_weight,
):
    groups, tps = lax.axis_size("grp"), lax.axis_size("tp")
    depth = groups // 4
    tokens, width = activations.shape
    own, kw = key_master.shape[1:]
    chunk = width // depth
    steps = decode_hidden.shape[1]
    cached, kv_cols = cache_keys.shape[1:]
    heads = kv_cols // HD
    hidden = decode_hidden.reshape(steps, -1)
    mine = lax.dynamic_slice_in_dim(hidden, lax.axis_index("tp") * width, width, 1)
    mine = mine.reshape(steps, depth, chunk).transpose(1, 0, 2).astype(F32)
    q_pad = -(-GQA * steps // 16) * 16
    vmem = pl.BlockSpec(memory_space=pltpu.VMEM)
    anywhere = pl.BlockSpec(memory_space=pl.ANY)
    smem = pl.BlockSpec(memory_space=pltpu.SMEM)
    dma = pltpu.SemaphoreType.DMA
    rows = groups * steps
    outs = pl.pallas_call(
        functools.partial(fused, (groups, tps, steps)),
        out_shape=(
            jax.ShapeDtypeStruct((own, kw), F32),
            jax.ShapeDtypeStruct((own, kw), F32),
            jax.ShapeDtypeStruct((own, kw), F32),
            jax.ShapeDtypeStruct((steps, kv_cols), BF16),
            jax.ShapeDtypeStruct((steps, kv_cols), BF16),
            jax.ShapeDtypeStruct((steps, queries.shape[2]), BF16),
        ),
        in_specs=[vmem] * 10 + [anywhere, anywhere, smem, anywhere],
        out_specs=(vmem,) * 6,
        scratch_shapes=[
            pltpu.VMEM((depth, 2, 2, own, kw), F32),
            pltpu.VMEM((depth, 2, own, kw), F32),
            pltpu.VMEM((depth, own, kw), F32),
            pltpu.VMEM((depth, own, kw), BF16),
            pltpu.VMEM((depth, own, kw), BF16),
            pltpu.VMEM((depth - 1, own, kw), BF16),
            pltpu.VMEM((depth - 1, own, kw), BF16),
            pltpu.VMEM((2, 2, depth, steps, chunk), F32),
            pltpu.VMEM((rows, chunk), F32),
            pltpu.VMEM((chunk, kw), BF16),
            pltpu.VMEM((rows // 2, kw), F32),
            pltpu.VMEM((rows // 2, kw), F32),
            pltpu.VMEM((rows // 4, kw), F32),
            pltpu.VMEM((rows // 4, kw), F32),
            pltpu.VMEM((depth - 1, steps, kw), F32),
            pltpu.VMEM((depth - 1, steps, kw), F32),
            pltpu.VMEM((tps, steps, kw // tps), F32),
            pltpu.VMEM((tps - 1, steps, kw // tps), F32),
            pltpu.VMEM((cached, kv_cols), BF16),
            pltpu.VMEM((cached, kv_cols), BF16),
            pltpu.VMEM(value_weight.shape, BF16),
            pltpu.VMEM((heads, q_pad, HD), F32),
            pltpu.VMEM((heads, q_pad, cached), F32),
            pltpu.VMEM((HD, kv_cols), BF16),
            pltpu.VMEM((HD, kv_cols), BF16),
            pltpu.VMEM((16, kv_cols), F32),
            pltpu.VMEM((steps, queries.shape[2]), F32),
            dma((3,)),
            dma((2, depth)),
            dma((2, depth)),
            dma((2, depth)),
            dma((2, depth)),
            dma((2, 2)),
            dma((2, 2)),
            dma((2, depth)),
            dma((2, tps)),
        ],
        compiler_params=pltpu.CompilerParams(
            collective_id=0, has_side_effects=True, vmem_limit_bytes=56 * 1024 * 1024
        ),
        cost_estimate=pl.CostEstimate(
            flops=2 * tokens * width * kw, bytes_accessed=8 * width * kw, transcendentals=0
        ),
    )(
        activations,
        cotangent,
        advantage.reshape(1, -1),
        seq_len.reshape(1, -1),
        key_master[0],
        moment_one[0],
        moment_two[0],
        mine,
        hidden,
        queries[0],
        cache_keys[0],
        cache_values[0],
        cache_len,
        value_weight,
    )
    outs = pl.pallas_call(
        hand_over,
        out_shape=tuple(jax.ShapeDtypeStruct(out.shape, out.dtype) for out in outs),
        in_specs=[vmem] * 6,
        out_specs=(vmem,) * 6,
    )(*outs)
    return tuple(out[None] for out in outs)


def fits(activations, key_master, decode_hidden, cache_keys, value_weight):
    groups, tps = lax.axis_size("grp"), lax.axis_size("tp")
    own = key_master.shape[1]
    return (
        groups % 4 == 0
        and groups >= 8
        and tps >= 2
        and own % 16 == 0
        and own * groups == activations.shape[1]
        and (4 * own) % 128 == 0
        and decode_hidden.shape[0] == 1
        and decode_hidden.shape[1] <= 16
        and cache_keys.shape[1] % 128 == 0
    )


def shards(*args):
    if fits(args[0], args[4], args[7], args[9], args[12]):
        return fast_shards(*args)
    return plain_shards(*args)


def solution(mesh):
    placed = (
        P("grp", "tp"),
        P("grp", None),
        P(),
        P(),
        P("tp", "grp", None),
        P("tp", "grp", None),
        P("tp", "grp", None),
        P("grp", None, None),
        P("grp", None, "tp"),
        P("grp", None, "tp"),
        P("grp", None, "tp"),
        P("grp"),
        P(None, "tp"),
    )
    return jax.shard_map(
        shards,
        mesh=mesh,
        in_specs=placed,
        out_specs=(
            P("tp", "grp", None),
            P("tp", "grp", None),
            P("tp", "grp", None),
            P("grp", None, "tp"),
            P("grp", None, "tp"),
            P("grp", None, "tp"),
        ),
        check_vma=False,
    )
```
